32 devices in a mesh: grp: 2 (over y), wide: 8 (over z, x), tm: 2 (over core).
Axes of the slice: x: 2, y: 2, z: 4, core: 2. Of those that a mesh axis runs over, the one named last changes fastest.
Arguments:
- voltages: bfloat16 [2048, 65536], P('wide', ('grp', 'tm')), parts along dimension 1, may hold values from -6 to 6
- channels: int32 [16], replicated, may hold values from 0 to 1023, as said below
- tile_pairs: int32 [128, 2], replicated, may hold values from 0 to 31, as said below
Outputs:
- visibility: bfloat16 [32, 128, 64, 128], P(('grp', 'wide', 'tm')), parts along dimension 0
The draws below stay inside these ranges and needn't reach their ends.
There are 2 independent parts, one for each index of `grp`. The reference program is written for one: setup_inputs(seed, part) draws one part's arguments, and reference() takes and returns one part's arrays. A program takes and returns all parts, laid end to end along the dimension named above; an argument that names none is the same for every part. Nothing has to cross between parts.
Inputs may be any that keep to these rules, and one draw needn't show every extreme that they name: `channels`: 16 different channel numbers in no fixed order; 0 and 1023 are always among them. `tile_pairs`: 128 different ordered tile pairs; (0, 0) and (31, 31) are always among them.
All inputs are finite; a program needn't handle non-finite values.
Results may differ from the reference program's by a relative error of at most 0.0071.
Values may be sent and summed in bfloat16 or wider, within the bound.
No kernel may reach another device: no remote copies, remote signals or barrier semaphores. Data moves between devices by JAX's collectives and lax.ppermute only.
A program may use at most 64 MiB of HBM per device.

```python
import jax
import jax.numpy as jnp
from jax import lax

INPUTS = 2048
TILE = 64
NFFT = 2048
NCHAN = 1024
TILES = 32
NPAIR = 128
FRAMES = 16
SEL = 16


def draw_channels(key, part):
    interior = jax.random.permutation(key, jnp.arange(1, NCHAN - 1, dtype=jnp.int32))[:SEL - 2]
    picked = jnp.concatenate([interior, jnp.array([0, NCHAN - 1], dtype=jnp.int32)])
    return jax.random.permutation(jax.random.fold_in(key, 7), picked)


def draw_tile_pairs(key, part):
    interior = jax.random.permutation(key, jnp.arange(1, TILES * TILES - 1, dtype=jnp.int32))[:NPAIR - 2]
    picked = jnp.concatenate([interior, jnp.array([0, TILES * TILES - 1], dtype=jnp.int32)])
    picked = jax.random.permutation(jax.random.fold_in(key, 11), picked)
    return jnp.stack([picked // TILES, picked % TILES], 1)


def block_levels(own_key, dims, cuts, low, high):
    gain = 1.0
    for position, parts in cuts:
        draws = jax.random.uniform(jax.random.fold_in(jax.random.fold_in(own_key, 6), position), (parts,), jnp.float32, low / len(cuts), high / len(cuts))
        gain = gain * jnp.repeat(jnp.exp(draws), dims[position] // parts).reshape((-1,) + (1,) * (len(dims) - 1 - position))
    return gain


def normal_values(stream_key, shape, deviation, most, cuts=(), kind=jnp.bfloat16):
    factor_of = block_levels(stream_key, shape, cuts, -0.22, 0.18) if cuts else 1.0
    drawn = jax.random.normal(stream_key, shape, jnp.float32) * deviation * factor_of
    return jnp.minimum(jnp.maximum(drawn, -most), most).astype(kind)


def setup_inputs(seed: int = 0, part: int = 0) -> dict:
    key_list = jax.random.split(jax.random.key(seed), 4)
    part_splits = jax.random.split(jax.random.fold_in(key_list[3], part), 4)
    return {
        "voltages": normal_values(part_splits[0], (INPUTS, FRAMES * NFFT), 1.0, 6.0, ((0, 8), (1, 2))),
        "channels": draw_channels(jax.random.fold_in(key_list[3], 71), part),
        "tile_pairs": draw_tile_pairs(jax.random.fold_in(key_list[3], 71), part),
    }


def dft_table(channels, length):
    samples = jnp.arange(length, dtype=jnp.int32)
    phase = channels[:, None] * samples[None, :] % length
    angle = 2.0 * jnp.pi / length * phase.astype(jnp.float32)
    window = 0.5 - 0.5 * jnp.cos(2.0 * jnp.pi / length * samples.astype(jnp.float32))
    scale = 1.0 / jnp.sqrt(jnp.float32(0.375 * length))
    table = jnp.concatenate([window * jnp.cos(angle), -window * jnp.sin(angle)], 0) * scale
    return table.astype(jnp.bfloat16)

def reference(voltages, channels, tile_pairs):
    table = dft_table(channels, NFFT)
    blocks = voltages.reshape(INPUTS // TILE, TILE * FRAMES, NFFT)

    def transform(block):
        return jnp.dot(table, block.T, preferred_element_type=jnp.float32).astype(jnp.bfloat16)
    spectra = lax.map(transform, blocks)
    spectra = spectra.reshape(INPUTS // TILE, 2, SEL, TILE, FRAMES)
    spectra = spectra.transpose(2, 1, 0, 3, 4).reshape(SEL, 2, INPUTS, FRAMES)

    def one_channel(spec):

        def one_pair(pair):
            first = lax.dynamic_slice_in_dim(spec, (pair[0] * TILE).astype(jnp.int32), TILE, 1).reshape(2 * TILE, FRAMES)
            second = lax.dynamic_slice_in_dim(spec, (pair[1] * TILE).astype(jnp.int32), TILE, 1).reshape(2 * TILE, FRAMES)
            prod = jnp.dot(first, second.T, preferred_element_type=jnp.float32)
            real = prod[:TILE, :TILE] + prod[TILE:, TILE:]
            imag = prod[:TILE, TILE:] - prod[TILE:, :TILE]
            return (jnp.concatenate([real, imag], 1) / FRAMES).astype(jnp.bfloat16)
        return lax.map(one_pair, tile_pairs)
    return lax.map(one_channel, spectra)
```

```python
import functools
import math

import jax
import jax.numpy as jnp
from jax import lax
from jax.experimental import pallas as pl
from jax.experimental.pallas import tpu as pltpu
from jax.sharding import PartitionSpec as P

TILE = 64
NFFT = 2048
LANES = 128
VMEM_LIMIT = 48 * 1024 * 1024


def cos_sin(phase):
    quarter = NFFT // 4
    turn = (phase + quarter // 2) // quarter
    x = (phase - turn * quarter).astype(jnp.float32) * (2.0 * math.pi / NFFT)
    y = x * x
    c = 1.0 + y * (-1 / 2 + y * (1 / 24 + y * (-1 / 720 + y * (1 / 40320))))
    s = x * (1.0 + y * (-1 / 6 + y * (1 / 120 + y * (-1 / 5040 + y * (1 / 362880)))))
    odd = (turn & 1) == 1
    cos = jnp.where(odd, s, c)
    sin = jnp.where(odd, c, s)
    cos = jnp.where(((turn + 1) & 2) == 2, -cos, cos)
    sin = jnp.where((turn & 2) == 2, -sin, sin)
    return cos, sin


def fill_table(chan_ref, table):
    count = table.shape[0] // 2
    rows = lax.broadcasted_iota(jnp.int32, (count, LANES), 0)
    chan = jnp.zeros((count, LANES), jnp.int32)
    for s in range(count):
        chan = jnp.where(rows == s, chan_ref[s], chan)
    lane = lax.broadcasted_iota(jnp.int32, (count, LANES), 1)
    scale = 1.0 / math.sqrt(0.375 * NFFT)
    for start in range(0, NFFT, LANES):
        n = lane + start
        window = 0.5 - 0.5 * cos_sin(n[:8])[0]
        window = jnp.tile(window * scale, (count // 8, 1))
        cos, sin = cos_sin((chan * n) & (NFFT - 1))
        table[:count, start : start + LANES] = (window * cos).astype(table.dtype)
        table[count:, start : start + LANES] = (-window * sin).astype(table.dtype)


def spectra_kernel(chan_hbm, volt_hbm, out_ref, chan, volt, table, spec, chan_sem, sems):
    frames = volt.shape[0]
    count = spec.shape[0]
    chan_copy = pltpu.make_async_copy(chan_hbm, chan, chan_sem)
    chan_copy.start()
    copies = []
    for f in range(frames):
        copy = pltpu.make_async_copy(
            volt_hbm.at[:, f * NFFT : (f + 1) * NFFT], volt.at[f], sems.at[f]
        )
        copy.start()
        copies.append(copy)
    chan_copy.wait()
    fill_table(chan, table)
    for f in range(frames):
        copies[f].wait()
        result = lax.dot_general(
            table[...], volt[f], (((1,), (1,)), ((), ())), preferred_element_type=jnp.float32
        )
        spec[:, f, :] = result[:count]
        spec[:, frames + f, :] = result[count:]
    out_ref[...] = spec[...].astype(out_ref.dtype)


def spectra_of(voltages, channels):
    in_dev = voltages.shape[0]
    frames = voltages.shape[1] // NFFT
    count = channels.shape[0]
    return pl.pallas_call(
        spectra_kernel,
        out_shape=jax.ShapeDtypeStruct((count, 2 * frames, in_dev), jnp.bfloat16),
        in_specs=[pl.BlockSpec(memory_space=pl.ANY)] * 2,
        out_specs=pl.BlockSpec(memory_space=pltpu.VMEM),
        scratch_shapes=[
            pltpu.SMEM((count,), jnp.int32),
            pltpu.VMEM((frames, in_dev, NFFT), voltages.dtype),
            pltpu.VMEM((2 * count, NFFT), jnp.bfloat16),
            pltpu.VMEM((count, 2 * frames, in_dev), jnp.float32),
            pltpu.SemaphoreType.DMA,
            pltpu.SemaphoreType.DMA((frames,)),
        ],
        compiler_params=pltpu.CompilerParams(vmem_limit_bytes=VMEM_LIMIT),
        name="spectra",
    )(channels, voltages)


def pairs_kernel(scale, pairs_ref, turned_ref, out_hbm, left, right, out, sems):
    blocks, times, rows, width = turned_ref.shape
    half = rows // 2
    depth = times * rows
    low = lax.broadcasted_iota(jnp.int32, (rows, LANES), 1) < TILE
    per_lane = LANES // TILE
    for w in range(blocks):
        stacks = []
        for t in range(times):
            x = turned_ref[w, t].astype(jnp.float32)
            stacks.append(x)
            m = jnp.concatenate([x[half:], -x[:half]], 0)
            for c in range(width // LANES):
                xc = x[:, c * LANES : (c + 1) * LANES]
                mc = m[:, c * LANES : (c + 1) * LANES]
                tile = w * (width // TILE) + c * per_lane
                even = jnp.where(low, xc, pltpu.roll(mc, TILE, 1))
                odd = jnp.where(low, pltpu.roll(xc, TILE, 1), mc)
                right[tile, t * rows : (t + 1) * rows] = even.astype(right.dtype)
                right[tile + 1, t * rows : (t + 1) * rows] = odd.astype(right.dtype)
        stack = jnp.concatenate(stacks, 0)
        for u in range(width // LANES):
            turned = stack[:, u * LANES : (u + 1) * LANES].T.astype(left.dtype)
            tile = w * (width // TILE) + u * per_lane
            left[tile] = turned[:TILE]
            left[tile + 1] = turned[TILE:]

    npairs = out.shape[0]
    parts = sems.shape[0]
    step = npairs // parts
    copies = []
    for part in range(parts):

        @pl.loop(0, step, unroll=8)
        def _(i):
            p = part * step + i
            prod = lax.dot_general(
                left[pairs_ref[2 * p]],
                right[pairs_ref[2 * p + 1]],
                (((1,), (0,)), ((), ())),
                preferred_element_type=jnp.float32,
            )
            out[p] = (prod * scale).astype(out.dtype)

        span = pl.ds(part * step, step)
        copy = pltpu.make_async_copy(out.at[span], out_hbm.at[span], sems.at[part])
        copy.start()
        copies.append(copy)
    for copy in copies:
        copy.wait()


def products_of(turned, tile_pairs, frames_all):
    blocks, times, rows, width = turned.shape
    npairs = tile_pairs.shape[0]
    tiles = blocks * width // TILE
    depth = times * rows
    return pl.pallas_call(
        functools.partial(pairs_kernel, 1.0 / frames_all),
        out_shape=jax.ShapeDtypeStruct((npairs, TILE, 2 * TILE), jnp.bfloat16),
        in_specs=[
            pl.BlockSpec(memory_space=pltpu.SMEM),
            pl.BlockSpec(memory_space=pltpu.VMEM),
        ],
        out_specs=pl.BlockSpec(memory_space=pl.ANY),
        scratch_shapes=[
            pltpu.VMEM((tiles, TILE, depth), jnp.bfloat16),
            pltpu.VMEM((tiles, depth, 2 * TILE), jnp.bfloat16),
            pltpu.VMEM((npairs, TILE, 2 * TILE), jnp.bfloat16),
            pltpu.SemaphoreType.DMA((4,)),
        ],
        compiler_params=pltpu.CompilerParams(vmem_limit_bytes=VMEM_LIMIT),
        name="pair_products",
    )(tile_pairs.reshape(-1), turned)


def shards(voltages, channels, tile_pairs):
    n_wide = lax.axis_size("wide")
    n_time = lax.axis_size("tm")
    in_dev = voltages.shape[0]
    frames_dev = voltages.shape[1] // NFFT
    count = channels.shape[0]
    per_dev = count // (n_wide * n_time)
    rows = 2 * frames_dev

    spectra = spectra_of(voltages, channels)
    turned = lax.all_to_all(spectra, ("wide", "tm"), split_axis=0, concat_axis=0, tiled=True)
    turned = turned.reshape(n_wide, n_time, per_dev, rows, in_dev)
    results = []
    for c in range(per_dev):
        one = turned[:, :, c]
        if in_dev % LANES:
            one = one.transpose(1, 2, 0, 3).reshape(1, n_time, rows, n_wide * in_dev)
        results.append(products_of(one, tile_pairs, frames_dev * n_time))
    return jnp.stack(results)


def solution(mesh):
    return jax.shard_map(
        shards,
        mesh=mesh,
        in_specs=(P("wide", ("grp", "tm")), P(), P()),
        out_specs=P(("grp", "wide", "tm"), None, None, None),
        check_vma=False,
    )
```

```python
import functools
import math

import jax
import jax.numpy as jnp
from jax import lax
from jax.experimental import pallas as pl
from jax.experimental.pallas import tpu as pltpu
from jax.sharding import PartitionSpec as P

TILE = 64
NFFT = 2048
LANES = 128
VMEM_LIMIT = 48 * 1024 * 1024


def divisor(n, most):
    return max(d for d in range(1, most + 1) if n % d == 0)


def cos_sin(phase):
    quarter = NFFT // 4
    turn = (phase + quarter // 2) // quarter
    x = (phase - turn * quarter).astype(jnp.float32) * (2.0 * math.pi / NFFT)
    y = x * x
    c = 1.0 + y * (-1 / 2 + y * (1 / 24 + y * (-1 / 720 + y * (1 / 40320))))
    s = x * (1.0 + y * (-1 / 6 + y * (1 / 120 + y * (-1 / 5040 + y * (1 / 362880)))))
    odd = (turn & 1) == 1
    cos = jnp.where(odd, s, c)
    sin = jnp.where(odd, c, s)
    cos = jnp.where(((turn + 1) & 2) == 2, -cos, cos)
    sin = jnp.where((turn & 2) == 2, -sin, sin)
    return cos, sin


def fill_table(order, chan_ref, table):
    count = table.shape[0] // 2
    rows = lax.broadcasted_iota(jnp.int32, (count, LANES), 0)
    chan = jnp.zeros((count, LANES), jnp.int32)
    for s in range(count):
        chan = jnp.where(rows == s, chan_ref[order[s]], chan)
    lane = lax.broadcasted_iota(jnp.int32, (count, LANES), 1)
    scale = 1.0 / math.sqrt(0.375 * NFFT)

    @pl.loop(0, NFFT // LANES)
    def _(j):
        start = pl.multiple_of(j * LANES, LANES)
        n = lane + start
        window = 0.5 - 0.5 * cos_sin(n[:8])[0]
        window = jnp.tile(window * scale, (count // 8, 1))
        cos, sin = cos_sin((chan * n) & (NFFT - 1))
        table[:count, pl.ds(start, LANES)] = (window * cos).astype(table.dtype)
        table[count:, pl.ds(start, LANES)] = (-window * sin).astype(table.dtype)


def spectra_kernel(order, chan_hbm, volt_hbm, out_ref, chan, volt, table, spec, chan_sem, sems):
    frames, in_dev = volt.shape[:2]
    count = spec.shape[0]

    def frame(f):
        start = pl.multiple_of(f * NFFT, NFFT)
        return pltpu.make_async_copy(volt_hbm.at[:, pl.ds(start, NFFT)], volt.at[f], sems.at[f])

    chan_copy = pltpu.make_async_copy(chan_hbm, chan, chan_sem)
    chan_copy.start()

    @pl.loop(0, frames)
    def _(f):
        frame(f).start()

    chan_copy.wait()
    fill_table(order, chan, table)

    @pl.loop(0, frames)
    def _(f):
        frame(f).wait()
        result = lax.dot_general(
            table[...], volt[f], (((1,), (1,)), ((), ())), preferred_element_type=jnp.float32
        )
        spec[:, pl.ds(f, 1), :] = result[:count].reshape(count, 1, in_dev)
        spec[:, pl.ds(frames + f, 1), :] = result[count:].reshape(count, 1, in_dev)

    out_ref[...] = spec[...].astype(out_ref.dtype)


def spectra_of(voltages, channels, order):
    in_dev = voltages.shape[0]
    frames = voltages.shape[1] // NFFT
    count = channels.shape[0]
    return pl.pallas_call(
        functools.partial(spectra_kernel, order),
        out_shape=jax.ShapeDtypeStruct((count, 2 * frames, in_dev), jnp.bfloat16),
        in_specs=[pl.BlockSpec(memory_space=pl.ANY)] * 2,
        out_specs=pl.BlockSpec(memory_space=pltpu.VMEM),
        scratch_shapes=[
            pltpu.SMEM((count,), jnp.int32),
            pltpu.VMEM((frames, in_dev, NFFT), voltages.dtype),
            pltpu.VMEM((2 * count, NFFT), jnp.bfloat16),
            pltpu.VMEM((count, 2 * frames, in_dev), jnp.float32),
            pltpu.SemaphoreType.DMA,
            pltpu.SemaphoreType.DMA((frames,)),
        ],
        compiler_params=pltpu.CompilerParams(vmem_limit_bytes=VMEM_LIMIT),
        name="spectra",
    )(pltpu.with_memory_space_constraint(channels, pltpu.HBM), voltages)


def pairs_kernel(scale, places, pairs_ref, turned_ref, out_hbm, left, right, out, sems):
    sources, rows, width = turned_ref.shape
    times = len(places[0])
    half = rows // 2
    low = lax.broadcasted_iota(jnp.int32, (rows, LANES), 1) < TILE
    for w, place in enumerate(places):
        stack = []
        for t in range(times):
            x = turned_ref[place[t]].astype(jnp.float32)
            stack.append(x)
            m = jnp.concatenate([x[half:], -x[:half]], 0)
            for u in range(width // LANES):
                xu = x[:, u * LANES : (u + 1) * LANES]
                mu = m[:, u * LANES : (u + 1) * LANES]
                tile = (w * width + u * LANES) // TILE
                depth = slice(t * rows, (t + 1) * rows)
                first = jnp.where(low, xu, pltpu.roll(mu, TILE, 1))
                second = jnp.where(low, pltpu.roll(xu, TILE, 1), mu)
                right[tile, depth] = first.astype(right.dtype)
                right[tile + 1, depth] = second.astype(right.dtype)
        stack = jnp.concatenate(stack, 0)
        for u in range(width // LANES):
            turned = stack[:, u * LANES : (u + 1) * LANES].T.astype(left.dtype)
            tile = (w * width + u * LANES) // TILE
            left[tile] = turned[:TILE]
            left[tile + 1] = turned[TILE:]

    parts = sems.shape[0]
    step = out.shape[0] // parts

    def part(i):
        span = pl.ds(i * step, step)
        return pltpu.make_async_copy(out.at[span], out_hbm.at[span], sems.at[i])

    @pl.loop(0, parts)
    def _(i):
        for k in range(step):
            p = i * step + k
            product = lax.dot_general(
                left[pairs_ref[2 * p]],
                right[pairs_ref[2 * p + 1]],
                (((1,), (0,)), ((), ())),
                preferred_element_type=jnp.float32,
            )
            out[p] = (product * scale).astype(out.dtype)
        part(i).start()

    @pl.loop(0, parts)
    def _(i):
        part(i).wait()


def products_of(turned, places, tile_pairs, frames_all):
    sources, rows, width = turned.shape
    npairs = tile_pairs.shape[0]
    depth = len(places[0]) * rows
    tiles = len(places) * width // TILE
    return pl.pallas_call(
        functools.partial(pairs_kernel, 1.0 / frames_all, places),
        out_shape=jax.ShapeDtypeStruct((npairs, TILE, 2 * TILE), jnp.bfloat16),
        in_specs=[
            pl.BlockSpec(memory_space=pltpu.SMEM),
            pl.BlockSpec(memory_space=pltpu.VMEM),
        ],
        out_specs=pl.BlockSpec(memory_space=pl.ANY),
        scratch_shapes=[
            pltpu.VMEM((tiles, TILE, depth), jnp.bfloat16),
            pltpu.VMEM((tiles, depth, 2 * TILE), jnp.bfloat16),
            pltpu.VMEM((npairs, TILE, 2 * TILE), jnp.bfloat16),
            pltpu.SemaphoreType.DMA((npairs // divisor(npairs, 32),)),
        ],
        compiler_params=pltpu.CompilerParams(vmem_limit_bytes=VMEM_LIMIT),
        name="pair_products",
    )(tile_pairs.reshape(-1), turned)


def shards(voltages, channels, tile_pairs):
    n_wide = lax.axis_size("wide")
    n_time = lax.axis_size("tm")
    n_dev = n_wide * n_time
    in_dev = voltages.shape[0]
    frames_dev = voltages.shape[1] // NFFT
    count = channels.shape[0]
    per_dev = count // n_dev
    rows = 2 * frames_dev

    middle = n_wide // 2 * n_time + n_time - 1
    group = [middle] + [d for d in range(n_dev) if d != middle]
    place = {d: j for j, d in enumerate(group)}
    order = [d * per_dev + c for d in group for c in range(per_dev)]

    spectra = spectra_of(voltages, channels, order)
    turned = lax.all_to_all(
        spectra, ("wide", "tm"), split_axis=0, concat_axis=0, axis_index_groups=[group], tiled=True
    )
    turned = turned.reshape(n_dev, per_dev, rows, in_dev)
    results = []
    for c in range(per_dev):
        one = turned[:, c]
        places = [[place[w * n_time + t] for t in range(n_time)] for w in range(n_wide)]
        if in_dev % LANES:
            one = jnp.concatenate([one[1 : middle + 1], one[:1], one[middle + 1 :]], 0)
            one = one.reshape(n_wide, n_time, rows, in_dev).transpose(1, 2, 0, 3)
            one = one.reshape(n_time, rows, n_wide * in_dev)
            places = [list(range(n_time))]
        results.append(products_of(one, places, tile_pairs, frames_dev * n_time))
    return jnp.stack(results)


def solution(mesh):
    return jax.shard_map(
        shards,
        mesh=mesh,
        in_specs=(P("wide", ("grp", "tm")), P(), P()),
        out_specs=P(("grp", "wide", "tm"), None, None, None),
        check_vma=False,
    )
```

```python
import functools
import math

import jax
import jax.numpy as jnp
from jax import lax
from jax.experimental import pallas as pl
from jax.experimental.pallas import tpu as pltpu
from jax.sharding import PartitionSpec as P

TILE = 64
NFFT = 2048
LANES = 128
VMEM_LIMIT = 48 * 1024 * 1024


def divisor(n, most):
    return max(d for d in range(1, most + 1) if n % d == 0)


def cos_sin(phase):
    quarter = NFFT // 4
    turn = (phase + quarter // 2) // quarter
    x = (phase - turn * quarter).astype(jnp.float32) * (2.0 * math.pi / NFFT)
    y = x * x
    c = 1.0 + y * (-1 / 2 + y * (1 / 24 + y * (-1 / 720 + y * (1 / 40320))))
    s = x * (1.0 + y * (-1 / 6 + y * (1 / 120 + y * (-1 / 5040 + y * (1 / 362880)))))
    odd = (turn & 1) == 1
    cos = jnp.where(odd, s, c)
    sin = jnp.where(odd, c, s)
    cos = jnp.where(((turn + 1) & 2) == 2, -cos, cos)
    sin = jnp.where((turn & 2) == 2, -sin, sin)
    return cos, sin


def fill_table(order, chan_ref, table):
    count = table.shape[0] // 2
    rows = lax.broadcasted_iota(jnp.int32, (count, LANES), 0)
    chan = jnp.zeros((count, LANES), jnp.int32)
    for s in range(count):
        chan = jnp.where(rows == s, chan_ref[order[s]], chan)
    lane = lax.broadcasted_iota(jnp.int32, (count, LANES), 1)
    scale = 1.0 / math.sqrt(0.375 * NFFT)

    @pl.loop(0, NFFT // LANES)
    def _(j):
        start = pl.multiple_of(j * LANES, LANES)
        n = lane + start
        window = 0.5 - 0.5 * cos_sin(n[:8])[0]
        window = jnp.tile(window * scale, (count // 8, 1))
        cos, sin = cos_sin((chan * n) & (NFFT - 1))
        table[:count, pl.ds(start, LANES)] = (window * cos).astype(table.dtype)
        table[count:, pl.ds(start, LANES)] = (-window * sin).astype(table.dtype)


def spectra_kernel(order, chan_hbm, volt_hbm, out_ref, chan, volt, table, spec, chan_sem, sems):
    frames, in_dev = volt.shape[:2]
    count = spec.shape[0]

    def frame(f):
        start = pl.multiple_of(f * NFFT, NFFT)
        return pltpu.make_async_copy(volt_hbm.at[:, pl.ds(start, NFFT)], volt.at[f], sems.at[f])

    chan_copy = pltpu.make_async_copy(chan_hbm, chan, chan_sem)
    chan_copy.start()

    @pl.loop(0, frames)
    def _(f):
        frame(f).start()

    chan_copy.wait()
    fill_table(order, chan, table)

    @pl.loop(0, frames)
    def _(f):
        frame(f).wait()
        result = lax.dot_general(
            table[...], volt[f], (((1,), (1,)), ((), ())), preferred_element_type=jnp.float32
        )
        spec[:, pl.ds(f, 1), :] = result[:count].reshape(count, 1, in_dev)
        spec[:, pl.ds(frames + f, 1), :] = result[count:].reshape(count, 1, in_dev)

    out_ref[...] = spec[...].astype(out_ref.dtype)


def spectra_of(voltages, channels, order):
    in_dev = voltages.shape[0]
    frames = voltages.shape[1] // NFFT
    count = channels.shape[0]
    return pl.pallas_call(
        functools.partial(spectra_kernel, order),
        out_shape=jax.ShapeDtypeStruct((count, 2 * frames, in_dev), jnp.bfloat16),
        in_specs=[pl.BlockSpec(memory_space=pl.ANY)] * 2,
        out_specs=pl.BlockSpec(memory_space=pltpu.VMEM),
        scratch_shapes=[
            pltpu.SMEM((count,), jnp.int32),
            pltpu.VMEM((frames, in_dev, NFFT), voltages.dtype),
            pltpu.VMEM((2 * count, NFFT), jnp.bfloat16),
            pltpu.VMEM((count, 2 * frames, in_dev), jnp.float32),
            pltpu.SemaphoreType.DMA,
            pltpu.SemaphoreType.DMA((frames,)),
        ],
        compiler_params=pltpu.CompilerParams(vmem_limit_bytes=VMEM_LIMIT),
        name="spectra",
    )(pltpu.with_memory_space_constraint(channels, pltpu.HBM), voltages)


def pairs_kernel(scale, places, pairs_ref, turned_ref, out_hbm, left, right, out, sems):
    sources, rows, width = turned_ref.shape
    times = len(places[0])
    half = rows // 2
    low = lax.broadcasted_iota(jnp.int32, (rows, LANES), 1) < TILE
    for w, place in enumerate(places):
        stack = []
        for t in range(times):
            x = turned_ref[place[t]].astype(jnp.float32)
            stack.append(x)
            m = jnp.concatenate([x[half:], -x[:half]], 0)
            for u in range(width // LANES):
                xu = x[:, u * LANES : (u + 1) * LANES]
                mu = m[:, u * LANES : (u + 1) * LANES]
                tile = (w * width + u * LANES) // TILE
                depth = slice(t * rows, (t + 1) * rows)
                first = jnp.where(low, xu, pltpu.roll(mu, TILE, 1))
                second = jnp.where(low, pltpu.roll(xu, TILE, 1), mu)
                right[tile, depth] = first.astype(right.dtype)
                right[tile + 1, depth] = second.astype(right.dtype)
        stack = jnp.concatenate(stack, 0)
        for u in range(width // LANES):
            turned = stack[:, u * LANES : (u + 1) * LANES].T.astype(left.dtype)
            tile = (w * width + u * LANES) // TILE
            left[tile] = turned[:TILE]
            left[tile + 1] = turned[TILE:]

    parts = sems.shape[0]
    step = out.shape[0] // parts

    def part(i):
        span = pl.ds(i * step, step)
        return pltpu.make_async_copy(out.at[span], out_hbm.at[span], sems.at[i])

    @pl.loop(0, parts)
    def _(i):
        for k in range(step):
            p = i * step + k
            product = lax.dot_general(
                left[pairs_ref[2 * p]],
                right[pairs_ref[2 * p + 1]],
                (((1,), (0,)), ((), ())),
                preferred_element_type=jnp.float32,
            )
            out[p] = (product * scale).astype(out.dtype)
        part(i).start()

    @pl.loop(0, parts)
    def _(i):
        part(i).wait()


def products_of(turned, places, tile_pairs, frames_all):
    sources, rows, width = turned.shape
    npairs = tile_pairs.shape[0]
    depth = len(places[0]) * rows
    tiles = len(places) * width // TILE
    return pl.pallas_call(
        functools.partial(pairs_kernel, 1.0 / frames_all, places),
        out_shape=jax.ShapeDtypeStruct((npairs, TILE, 2 * TILE), jnp.bfloat16),
        in_specs=[
            pl.BlockSpec(memory_space=pltpu.SMEM),
            pl.BlockSpec(memory_space=pltpu.VMEM),
        ],
        out_specs=pl.BlockSpec(memory_space=pl.ANY),
        scratch_shapes=[
            pltpu.VMEM((tiles, TILE, depth), jnp.bfloat16),
            pltpu.VMEM((tiles, depth, 2 * TILE), jnp.bfloat16),
            pltpu.VMEM((npairs, TILE, 2 * TILE), jnp.bfloat16),
            pltpu.SemaphoreType.DMA((npairs // divisor(npairs, 32),)),
        ],
        compiler_params=pltpu.CompilerParams(vmem_limit_bytes=VMEM_LIMIT),
        name="pair_products",
    )(tile_pairs.reshape(-1), turned)


def turn_group(n_wide, n_time):
    middle = (n_wide // 2 + 1) * n_time - 1 + (n_time if n_wide > 2 else 0)
    plane = 2 * n_time
    others = [d for d in range(n_wide * n_time) if d != middle]
    return [middle] + sorted(others, key=lambda d: (-abs(d // plane - middle // plane), d))


def shards(voltages, channels, tile_pairs):
    n_wide = lax.axis_size("wide")
    n_time = lax.axis_size("tm")
    n_dev = n_wide * n_time
    in_dev = voltages.shape[0]
    frames_dev = voltages.shape[1] // NFFT
    count = channels.shape[0]
    per_dev = count // n_dev
    rows = 2 * frames_dev

    group = turn_group(n_wide, n_time)
    place = {d: j for j, d in enumerate(group)}
    order = [d * per_dev + c for d in group for c in range(per_dev)]

    spectra = spectra_of(voltages, channels, order)
    turned = lax.all_to_all(
        spectra, ("wide", "tm"), split_axis=0, concat_axis=0, axis_index_groups=[group], tiled=True
    )
    turned = turned.reshape(n_dev, per_dev, rows, in_dev)
    results = []
    for c in range(per_dev):
        one = turned[:, c]
        places = [[place[w * n_time + t] for t in range(n_time)] for w in range(n_wide)]
        if in_dev % LANES:
            one = jnp.take(one, jnp.array([place[d] for d in range(n_dev)]), axis=0)
            one = one.reshape(n_wide, n_time, rows, in_dev).transpose(1, 2, 0, 3)
            one = one.reshape(n_time, rows, n_wide * in_dev)
            places = [list(range(n_time))]
        results.append(products_of(one, places, tile_pairs, frames_dev * n_time))
    return jnp.stack(results)


def solution(mesh):
    return jax.shard_map(
        shards,
        mesh=mesh,
        in_specs=(P("wide", ("grp", "tm")), P(), P()),
        out_specs=P(("grp", "wide", "tm"), None, None, None),
        check_vma=False,
    )
```

```python
import functools
import math

import jax
import jax.numpy as jnp
from jax import lax
from jax.experimental import pallas as pl
from jax.experimental.pallas import tpu as pltpu
from jax.sharding import PartitionSpec as P

TILE = 64
NFFT = 2048
LANES = 128
VMEM_LIMIT = 48 * 1024 * 1024


def divisor(n, most):
    return max(d for d in range(1, most + 1) if n % d == 0)


def cos_sin(phase):
    quarter = NFFT // 4
    turn = (phase + quarter // 2) // quarter
    x = (phase - turn * quarter).astype(jnp.float32) * (2.0 * math.pi / NFFT)
    y = x * x
    c = 1.0 + y * (-1 / 2 + y * (1 / 24 + y * (-1 / 720 + y * (1 / 40320))))
    s = x * (1.0 + y * (-1 / 6 + y * (1 / 120 + y * (-1 / 5040 + y * (1 / 362880)))))
    odd = (turn & 1) == 1
    cos = jnp.where(odd, s, c)
    sin = jnp.where(odd, c, s)
    cos = jnp.where(((turn + 1) & 2) == 2, -cos, cos)
    sin = jnp.where((turn & 2) == 2, -sin, sin)
    return cos, sin


def fill_table(order, chan_ref, table):
    count = table.shape[0] // 2
    rows = lax.broadcasted_iota(jnp.int32, (count, LANES), 0)
    chan = jnp.zeros((count, LANES), jnp.int32)
    for s in range(count):
        chan = jnp.where(rows == s, chan_ref[order[s]], chan)
    lane = lax.broadcasted_iota(jnp.int32, (count, LANES), 1)
    scale = 1.0 / math.sqrt(0.375 * NFFT)

    @pl.loop(0, NFFT // LANES)
    def _(j):
        start = pl.multiple_of(j * LANES, LANES)
        n = lane + start
        window = 0.5 - 0.5 * cos_sin(n[:8])[0]
        window = jnp.tile(window * scale, (count // 8, 1))
        cos, sin = cos_sin((chan * n) & (NFFT - 1))
        table[:count, pl.ds(start, LANES)] = (window * cos).astype(table.dtype)
        table[count:, pl.ds(start, LANES)] = (-window * sin).astype(table.dtype)


def spectra_kernel(order, chan_hbm, volt_hbm, out_ref, chan, volt, table, spec, chan_sem, sems):
    frames, in_dev = volt.shape[:2]
    count = spec.shape[0]

    def frame(f):
        start = pl.multiple_of(f * NFFT, NFFT)
        return pltpu.make_async_copy(volt_hbm.at[:, pl.ds(start, NFFT)], volt.at[f], sems.at[f])

    chan_copy = pltpu.make_async_copy(chan_hbm, chan, chan_sem)
    chan_copy.start()

    @pl.loop(0, frames)
    def _(f):
        frame(f).start()

    chan_copy.wait()
    fill_table(order, chan, table)

    def transform(f, several):
        for k in range(several):
            frame(f + k).wait()
        block = volt[pl.ds(f, several)].reshape(several * in_dev, NFFT)
        result = lax.dot_general(
            table[...], block, (((1,), (1,)), ((), ())), preferred_element_type=jnp.float32
        )
        for k in range(several):
            part = result[:, k * in_dev : (k + 1) * in_dev]
            spec[:, pl.ds(f + k, 1), :] = part[:count].reshape(count, 1, in_dev)
            spec[:, pl.ds(frames + f + k, 1), :] = part[count:].reshape(count, 1, in_dev)

    singles = min(frames, 2 + frames % 2)

    @pl.loop(0, singles)
    def _(f):
        transform(f, 1)

    @pl.loop(0, (frames - singles) // 2)
    def _(g):
        transform(singles + 2 * g, 2)

    out_ref[...] = spec[...].astype(out_ref.dtype)


def spectra_of(voltages, channels, order):
    in_dev = voltages.shape[0]
    frames = voltages.shape[1] // NFFT
    count = channels.shape[0]
    return pl.pallas_call(
        functools.partial(spectra_kernel, order),
        out_shape=jax.ShapeDtypeStruct((count, 2 * frames, in_dev), jnp.bfloat16),
        in_specs=[pl.BlockSpec(memory_space=pl.ANY)] * 2,
        out_specs=pl.BlockSpec(memory_space=pltpu.VMEM),
        scratch_shapes=[
            pltpu.SMEM((count,), jnp.int32),
            pltpu.VMEM((frames, in_dev, NFFT), voltages.dtype),
            pltpu.VMEM((2 * count, NFFT), jnp.bfloat16),
            pltpu.VMEM((count, 2 * frames, in_dev), jnp.float32),
            pltpu.SemaphoreType.DMA,
            pltpu.SemaphoreType.DMA((frames,)),
        ],
        compiler_params=pltpu.CompilerParams(vmem_limit_bytes=VMEM_LIMIT),
        name="spectra",
    )(pltpu.with_memory_space_constraint(channels, pltpu.HBM), voltages)


def pairs_kernel(
    scale, places, pairs_any, turned_ref, out_hbm, pairs_ref, left, right, out, pairs_sem, sems
):
    pairs_copy = pltpu.make_async_copy(pairs_any, pairs_ref, pairs_sem)
    pairs_copy.start()
    sources, rows, width = turned_ref.shape
    times = len(places[0])
    half = rows // 2
    low = lax.broadcasted_iota(jnp.int32, (rows, LANES), 1) < TILE
    for w, place in enumerate(places):
        stack = []
        for t in range(times):
            x = turned_ref[place[t]].astype(jnp.float32)
            stack.append(x)
            m = jnp.concatenate([x[half:], -x[:half]], 0)
            for u in range(width // LANES):
                xu = x[:, u * LANES : (u + 1) * LANES]
                mu = m[:, u * LANES : (u + 1) * LANES]
                tile = (w * width + u * LANES) // TILE
                depth = slice(t * rows, (t + 1) * rows)
                first = jnp.where(low, xu, pltpu.roll(mu, TILE, 1))
                second = jnp.where(low, pltpu.roll(xu, TILE, 1), mu)
                right[tile, depth] = first.astype(right.dtype)
                right[tile + 1, depth] = second.astype(right.dtype)
        stack = jnp.concatenate(stack, 0)
        for u in range(width // LANES):
            turned = stack[:, u * LANES : (u + 1) * LANES].T.astype(left.dtype)
            tile = (w * width + u * LANES) // TILE
            left[tile] = turned[:TILE]
            left[tile + 1] = turned[TILE:]

    parts = sems.shape[0]
    step = out.shape[0] // parts
    pairs_copy.wait()
    copies = []
    for i in range(parts):
        span = slice(i * step, (i + 1) * step)
        for p in range(i * step, (i + 1) * step):
            product = lax.dot_general(
                left[pairs_ref[2 * p]],
                right[pairs_ref[2 * p + 1]],
                (((1,), (0,)), ((), ())),
                preferred_element_type=jnp.float32,
            )
            out[p] = (product * scale).astype(out.dtype)
        copies.append(pltpu.make_async_copy(out.at[span], out_hbm.at[span], sems.at[i]))
        copies[-1].start()
    for copy in copies:
        copy.wait()


def products_of(turned, places, tile_pairs, frames_all):
    sources, rows, width = turned.shape
    npairs = tile_pairs.shape[0]
    depth = len(places[0]) * rows
    tiles = len(places) * width // TILE
    return pl.pallas_call(
        functools.partial(pairs_kernel, 1.0 / frames_all, places),
        out_shape=jax.ShapeDtypeStruct((npairs, TILE, 2 * TILE), jnp.bfloat16),
        in_specs=[
            pl.BlockSpec(memory_space=pl.ANY),
            pl.BlockSpec(memory_space=pltpu.VMEM),
        ],
        out_specs=pl.BlockSpec(memory_space=pl.ANY),
        scratch_shapes=[
            pltpu.SMEM((2 * npairs,), jnp.int32),
            pltpu.VMEM((tiles, TILE, depth), jnp.bfloat16),
            pltpu.VMEM((tiles, depth, 2 * TILE), jnp.bfloat16),
            pltpu.VMEM((npairs, TILE, 2 * TILE), jnp.bfloat16),
            pltpu.SemaphoreType.DMA,
            pltpu.SemaphoreType.DMA((npairs // divisor(npairs, 32),)),
        ],
        compiler_params=pltpu.CompilerParams(vmem_limit_bytes=VMEM_LIMIT),
        name="pair_products",
    )(tile_pairs.reshape(-1), turned)


def turn_group(n_wide, n_time):
    middle = (n_wide // 2 + 1) * n_time - 1 + (n_time if n_wide > 2 else 0)
    plane = 2 * n_time
    others = [d for d in range(n_wide * n_time) if d != middle]
    return [middle] + sorted(others, key=lambda d: (-abs(d // plane - middle // plane), d))


def shards(voltages, channels, tile_pairs):
    n_wide = lax.axis_size("wide")
    n_time = lax.axis_size("tm")
    n_dev = n_wide * n_time
    in_dev = voltages.shape[0]
    frames_dev = voltages.shape[1] // NFFT
    count = channels.shape[0]
    per_dev = count // n_dev
    rows = 2 * frames_dev

    group = turn_group(n_wide, n_time)
    place = {d: j for j, d in enumerate(group)}
    order = [d * per_dev + c for d in group for c in range(per_dev)]

    spectra = spectra_of(voltages, channels, order)
    turned = lax.all_to_all(
        spectra, ("wide", "tm"), split_axis=0, concat_axis=0, axis_index_groups=[group], tiled=True
    )
    turned = turned.reshape(n_dev, per_dev, rows, in_dev)
    results = []
    for c in range(per_dev):
        one = turned[:, c]
        places = [[place[w * n_time + t] for t in range(n_time)] for w in range(n_wide)]
        if in_dev % LANES:
            one = jnp.take(one, jnp.array([place[d] for d in range(n_dev)]), axis=0)
            one = one.reshape(n_wide, n_time, rows, in_dev).transpose(1, 2, 0, 3)
            one = one.reshape(n_time, rows, n_wide * in_dev)
            places = [list(range(n_time))]
        results.append(products_of(one, places, tile_pairs, frames_dev * n_time))
    return jnp.stack(results)


def solution(mesh):
    return jax.shard_map(
        shards,
        mesh=mesh,
        in_specs=(P("wide", ("grp", "tm")), P(), P()),
        out_specs=P(("grp", "wide", "tm"), None, None, None),
        check_vma=False,
    )
```

```python
import functools
import math

import jax
import jax.numpy as jnp
from jax import lax
from jax.experimental import pallas as pl
from jax.experimental.pallas import tpu as pltpu
from jax.sharding import PartitionSpec as P

TILE = 64
NFFT = 2048
LANES = 128
VMEM_LIMIT = 48 * 1024 * 1024


def divisor(n, most):
    return max(d for d in range(1, most + 1) if n % d == 0)


def cos_sin(phase):
    quarter = NFFT // 4
    turn = (phase + quarter // 2) // quarter
    x = (phase - turn * quarter).astype(jnp.float32) * (2.0 * math.pi / NFFT)
    y = x * x
    c = 1.0 + y * (-1 / 2 + y * (1 / 24 + y * (-1 / 720 + y * (1 / 40320))))
    s = x * (1.0 + y * (-1 / 6 + y * (1 / 120 + y * (-1 / 5040 + y * (1 / 362880)))))
    odd = (turn & 1) == 1
    cos = jnp.where(odd, s, c)
    sin = jnp.where(odd, c, s)
    cos = jnp.where(((turn + 1) & 2) == 2, -cos, cos)
    sin = jnp.where((turn & 2) == 2, -sin, sin)
    return cos, sin


def fill_table(order, chan_ref, table):
    count = table.shape[0] // 2
    rows = lax.broadcasted_iota(jnp.int32, (count, LANES), 0)
    chan = jnp.zeros((count, LANES), jnp.int32)
    for s in range(count):
        chan = jnp.where(rows == s, chan_ref[order[s]], chan)
    lane = lax.broadcasted_iota(jnp.int32, (count, LANES), 1)
    scale = 1.0 / math.sqrt(0.375 * NFFT)

    @pl.loop(0, NFFT // LANES)
    def _(j):
        start = pl.multiple_of(j * LANES, LANES)
        n = lane + start
        window = 0.5 - 0.5 * cos_sin(n[:8])[0]
        window = jnp.tile(window * scale, (count // 8, 1))
        cos, sin = cos_sin((chan * n) & (NFFT - 1))
        table[:count, pl.ds(start, LANES)] = (window * cos).astype(table.dtype)
        table[count:, pl.ds(start, LANES)] = (-window * sin).astype(table.dtype)


def spectra_kernel(order, chan_hbm, volt_hbm, out_ref, chan, volt, table, spec, chan_sem, sems):
    frames, in_dev = volt.shape[:2]
    count = spec.shape[0]

    def frame(f):
        start = pl.multiple_of(f * NFFT, NFFT)
        return pltpu.make_async_copy(volt_hbm.at[:, pl.ds(start, NFFT)], volt.at[f], sems.at[f])

    chan_copy = pltpu.make_async_copy(chan_hbm, chan, chan_sem)
    chan_copy.start()

    @pl.loop(0, frames)
    def _(f):
        frame(f).start()

    chan_copy.wait()
    fill_table(order, chan, table)

    def transform(f, several):
        for k in range(several):
            frame(f + k).wait()
        block = volt[pl.ds(f, several)].reshape(several * in_dev, NFFT)
        result = lax.dot_general(
            table[...], block, (((1,), (1,)), ((), ())), preferred_element_type=jnp.float32
        )
        for k in range(several):
            part = result[:, k * in_dev : (k + 1) * in_dev]
            spec[:, pl.ds(f + k, 1), :] = part[:count].reshape(count, 1, in_dev)
            spec[:, pl.ds(frames + f + k, 1), :] = part[count:].reshape(count, 1, in_dev)

    singles = min(frames, 2 + frames % 2)

    @pl.loop(0, singles)
    def _(f):
        transform(f, 1)

    @pl.loop(0, (frames - singles) // 2)
    def _(g):
        transform(singles + 2 * g, 2)

    out_ref[...] = spec[...].astype(out_ref.dtype)


def spectra_of(voltages, channels, order):
    in_dev = voltages.shape[0]
    frames = voltages.shape[1] // NFFT
    count = channels.shape[0]
    return pl.pallas_call(
        functools.partial(spectra_kernel, order),
        out_shape=jax.ShapeDtypeStruct((count, 2 * frames, in_dev), jnp.bfloat16),
        in_specs=[pl.BlockSpec(memory_space=pl.ANY)] * 2,
        out_specs=pl.BlockSpec(memory_space=pltpu.VMEM),
        scratch_shapes=[
            pltpu.SMEM((count,), jnp.int32),
            pltpu.VMEM((frames, in_dev, NFFT), voltages.dtype),
            pltpu.VMEM((2 * count, NFFT), jnp.bfloat16),
            pltpu.VMEM((count, 2 * frames, in_dev), jnp.float32),
            pltpu.SemaphoreType.DMA,
            pltpu.SemaphoreType.DMA((frames,)),
        ],
        compiler_params=pltpu.CompilerParams(vmem_limit_bytes=VMEM_LIMIT),
        name="spectra",
    )(pltpu.with_memory_space_constraint(channels, pltpu.HBM), voltages)


def pairs_kernel(
    scale, places, pairs_any, turned_ref, out_hbm, pairs_ref, left, right, out, pairs_sem, sems
):
    pairs_copy = pltpu.make_async_copy(pairs_any, pairs_ref, pairs_sem)
    pairs_copy.start()
    sources, rows, width = turned_ref.shape
    times = len(places[0])
    half = rows // 2
    low = lax.broadcasted_iota(jnp.int32, (rows, LANES), 1) < TILE
    for w, place in enumerate(places):
        stack = []
        for t in range(times):
            x = turned_ref[place[t]].astype(jnp.float32)
            stack.append(x)
            m = jnp.concatenate([x[half:], -x[:half]], 0)
            for u in range(width // LANES):
                xu = x[:, u * LANES : (u + 1) * LANES]
                mu = m[:, u * LANES : (u + 1) * LANES]
                tile = (w * width + u * LANES) // TILE
                depth = slice(t * rows, (t + 1) * rows)
                first = jnp.where(low, xu, pltpu.roll(mu, TILE, 1))
                second = jnp.where(low, pltpu.roll(xu, TILE, 1), mu)
                right[tile, depth] = first.astype(right.dtype)
                right[tile + 1, depth] = second.astype(right.dtype)
        stack = jnp.concatenate(stack, 0)
        for u in range(width // LANES):
            turned = stack[:, u * LANES : (u + 1) * LANES].T.astype(left.dtype)
            tile = (w * width + u * LANES) // TILE
            left[tile] = turned[:TILE]
            left[tile + 1] = turned[TILE:]

    parts = sems.shape[0]
    step = out.shape[0] // parts
    pairs_copy.wait()
    copies = []
    for i in range(parts):
        span = slice(i * step, (i + 1) * step)
        for p in range(i * step, (i + 1) * step):
            product = lax.dot_general(
                left[pairs_ref[0, p]],
                right[pairs_ref[1, p]],
                (((1,), (0,)), ((), ())),
                preferred_element_type=jnp.float32,
            )
            out[p] = (product * scale).astype(out.dtype)
        copies.append(pltpu.make_async_copy(out.at[span], out_hbm.at[span], sems.at[i]))
        copies[-1].start()
    for copy in copies:
        copy.wait()


def products_of(turned, places, tile_pairs, frames_all):
    sources, rows, width = turned.shape
    npairs = tile_pairs.shape[0]
    depth = len(places[0]) * rows
    tiles = len(places) * width // TILE
    return pl.pallas_call(
        functools.partial(pairs_kernel, 1.0 / frames_all, places),
        out_shape=jax.ShapeDtypeStruct((npairs, TILE, 2 * TILE), jnp.bfloat16),
        in_specs=[
            pl.BlockSpec(memory_space=pl.ANY),
            pl.BlockSpec(memory_space=pltpu.VMEM),
        ],
        out_specs=pl.BlockSpec(memory_space=pl.ANY),
        scratch_shapes=[
            pltpu.SMEM((2, npairs), jnp.int32),
            pltpu.VMEM((tiles, TILE, depth), jnp.bfloat16),
            pltpu.VMEM((tiles, depth, 2 * TILE), jnp.bfloat16),
            pltpu.VMEM((npairs, TILE, 2 * TILE), jnp.bfloat16),
            pltpu.SemaphoreType.DMA,
            pltpu.SemaphoreType.DMA((npairs // divisor(npairs, 32),)),
        ],
        compiler_params=pltpu.CompilerParams(vmem_limit_bytes=VMEM_LIMIT),
        name="pair_products",
    )(tile_pairs.T, turned)


def turn_group(n_wide, n_time):
    middle = (n_wide // 2 + 1) * n_time - 1 + (n_time if n_wide > 2 else 0)
    plane = 2 * n_time
    others = [d for d in range(n_wide * n_time) if d != middle]
    return [middle] + sorted(others, key=lambda d: (-abs(d // plane - middle // plane), d))


def shards(voltages, channels, tile_pairs):
    n_wide = lax.axis_size("wide")
    n_time = lax.axis_size("tm")
    n_dev = n_wide * n_time
    in_dev = voltages.shape[0]
    frames_dev = voltages.shape[1] // NFFT
    count = channels.shape[0]
    per_dev = count // n_dev
    rows = 2 * frames_dev

    group = turn_group(n_wide, n_time)
    place = {d: j for j, d in enumerate(group)}
    order = [d * per_dev + c for d in group for c in range(per_dev)]

    spectra = spectra_of(voltages, channels, order)
    turned = lax.all_to_all(
        spectra, ("wide", "tm"), split_axis=0, concat_axis=0, axis_index_groups=[group], tiled=True
    )
    turned = turned.reshape(n_dev, per_dev, rows, in_dev)
    results = []
    for c in range(per_dev):
        one = turned[:, c]
        places = [[place[w * n_time + t] for t in range(n_time)] for w in range(n_wide)]
        if in_dev % LANES:
            one = jnp.take(one, jnp.array([place[d] for d in range(n_dev)]), axis=0)
            one = one.reshape(n_wide, n_time, rows, in_dev).transpose(1, 2, 0, 3)
            one = one.reshape(n_time, rows, n_wide * in_dev)
            places = [list(range(n_time))]
        results.append(products_of(one, places, tile_pairs, frames_dev * n_time))
    return jnp.stack(results)


def solution(mesh):
    return jax.shard_map(
        shards,
        mesh=mesh,
        in_specs=(P("wide", ("grp", "tm")), P(), P()),
        out_specs=P(("grp", "wide", "tm"), None, None, None),
        check_vma=False,
    )
```

```python
import functools
import math

import jax
import jax.numpy as jnp
from jax import lax
from jax.experimental import pallas as pl
from jax.experimental.pallas import tpu as pltpu
from jax.sharding import PartitionSpec as P

TILE = 64
NFFT = 2048
LANES = 128
VMEM_LIMIT = 48 * 1024 * 1024


def divisor(n, most):
    return max(d for d in range(1, most + 1) if n % d == 0)


def cos_sin(phase):
    quarter = NFFT // 4
    turn = (phase + quarter // 2) // quarter
    x = (phase - turn * quarter).astype(jnp.float32) * (2.0 * math.pi / NFFT)
    y = x * x
    c = 1.0 + y * (-1 / 2 + y * (1 / 24 + y * (-1 / 720 + y * (1 / 40320))))
    s = x * (1.0 + y * (-1 / 6 + y * (1 / 120 + y * (-1 / 5040 + y * (1 / 362880)))))
    odd = (turn & 1) == 1
    cos = jnp.where(odd, s, c)
    sin = jnp.where(odd, c, s)
    cos = jnp.where(((turn + 1) & 2) == 2, -cos, cos)
    sin = jnp.where((turn & 2) == 2, -sin, sin)
    return cos, sin


def fill_table(order, chan_ref, table):
    count = table.shape[0] // 2
    rows = lax.broadcasted_iota(jnp.int32, (count, LANES), 0)
    chan = jnp.zeros((count, LANES), jnp.int32)
    for s in range(count):
        chan = jnp.where(rows == s, chan_ref[order[s]], chan)
    lane = lax.broadcasted_iota(jnp.int32, (count, LANES), 1)
    scale = 1.0 / math.sqrt(0.375 * NFFT)

    @pl.loop(0, NFFT // LANES)
    def _(j):
        start = pl.multiple_of(j * LANES, LANES)
        n = lane + start
        window = 0.5 - 0.5 * cos_sin(n[:8])[0]
        window = jnp.tile(window * scale, (count // 8, 1))
        cos, sin = cos_sin((chan * n) & (NFFT - 1))
        table[:count, pl.ds(start, LANES)] = (window * cos).astype(table.dtype)
        table[count:, pl.ds(start, LANES)] = (-window * sin).astype(table.dtype)


def spectra_kernel(
    order, chan_hbm, pairs_hbm, volt_hbm, out_ref, pairs_ref, chan, volt, table, spec, list_sems, sems
):
    frames, in_dev = volt.shape[:2]
    count = spec.shape[0]

    def frame(f):
        start = pl.multiple_of(f * NFFT, NFFT)
        return pltpu.make_async_copy(volt_hbm.at[:, pl.ds(start, NFFT)], volt.at[f], sems.at[f])

    chan_copy = pltpu.make_async_copy(chan_hbm, chan, list_sems.at[0])
    chan_copy.start()
    pairs_copy = pltpu.make_async_copy(pairs_hbm, pairs_ref, list_sems.at[1])
    pairs_copy.start()

    @pl.loop(0, frames)
    def _(f):
        frame(f).start()

    chan_copy.wait()
    pairs_copy.wait()
    fill_table(order, chan, table)

    def transform(f, several):
        for k in range(several):
            frame(f + k).wait()
        block = volt[pl.ds(f, several)].reshape(several * in_dev, NFFT)
        result = lax.dot_general(
            table[...], block, (((1,), (1,)), ((), ())), preferred_element_type=jnp.float32
        )
        for k in range(several):
            part = result[:, k * in_dev : (k + 1) * in_dev]
            spec[:, pl.ds(f + k, 1), :] = part[:count].reshape(count, 1, in_dev)
            spec[:, pl.ds(frames + f + k, 1), :] = part[count:].reshape(count, 1, in_dev)

    singles = min(frames, 2 + frames % 2)

    @pl.loop(0, singles)
    def _(f):
        transform(f, 1)

    @pl.loop(0, (frames - singles) // 2)
    def _(g):
        transform(singles + 2 * g, 2)

    out_ref[...] = spec[...].astype(out_ref.dtype)


def spectra_of(voltages, channels, tile_pairs, order):
    in_dev = voltages.shape[0]
    frames = voltages.shape[1] // NFFT
    count = channels.shape[0]
    lists = [pltpu.with_memory_space_constraint(x, pltpu.HBM) for x in (channels, tile_pairs.T)]
    return pl.pallas_call(
        functools.partial(spectra_kernel, order),
        out_shape=(
            jax.ShapeDtypeStruct((count, 2 * frames, in_dev), jnp.bfloat16),
            pltpu.SMEM(lists[1].shape, jnp.int32),
        ),
        in_specs=[pl.BlockSpec(memory_space=pl.ANY)] * 3,
        out_specs=(
            pl.BlockSpec(memory_space=pltpu.VMEM),
            pl.BlockSpec(memory_space=pltpu.SMEM),
        ),
        scratch_shapes=[
            pltpu.SMEM((count,), jnp.int32),
            pltpu.VMEM((frames, in_dev, NFFT), voltages.dtype),
            pltpu.VMEM((2 * count, NFFT), jnp.bfloat16),
            pltpu.VMEM((count, 2 * frames, in_dev), jnp.float32),
            pltpu.SemaphoreType.DMA((2,)),
            pltpu.SemaphoreType.DMA((frames,)),
        ],
        compiler_params=pltpu.CompilerParams(vmem_limit_bytes=VMEM_LIMIT),
        name="spectra",
    )(*lists, voltages)


def pairs_kernel(scale, places, pairs_ref, turned_ref, out_hbm, left, right, out, sems):
    sources, rows, width = turned_ref.shape
    times = len(places[0])
    half = rows // 2
    low = lax.broadcasted_iota(jnp.int32, (rows, LANES), 1) < TILE
    for w, place in enumerate(places):
        stack = []
        for t in range(times):
            x = turned_ref[place[t]].astype(jnp.float32)
            stack.append(x)
            m = jnp.concatenate([x[half:], -x[:half]], 0)
            for u in range(width // LANES):
                xu = x[:, u * LANES : (u + 1) * LANES]
                mu = m[:, u * LANES : (u + 1) * LANES]
                tile = (w * width + u * LANES) // TILE
                depth = slice(t * rows, (t + 1) * rows)
                first = jnp.where(low, xu, pltpu.roll(mu, TILE, 1))
                second = jnp.where(low, pltpu.roll(xu, TILE, 1), mu)
                right[tile, depth] = first.astype(right.dtype)
                right[tile + 1, depth] = second.astype(right.dtype)
        stack = jnp.concatenate(stack, 0)
        for u in range(width // LANES):
            turned = stack[:, u * LANES : (u + 1) * LANES].T.astype(left.dtype)
            tile = (w * width + u * LANES) // TILE
            left[tile] = turned[:TILE]
            left[tile + 1] = turned[TILE:]

    parts = sems.shape[0]
    step = out.shape[0] // parts
    copies = []
    for i in range(parts):
        span = slice(i * step, (i + 1) * step)
        for p in range(i * step, (i + 1) * step):
            product = lax.dot_general(
                left[pairs_ref[0, p]],
                right[pairs_ref[1, p]],
                (((1,), (0,)), ((), ())),
                preferred_element_type=jnp.float32,
            )
            out[p] = (product * scale).astype(out.dtype)
        copies.append(pltpu.make_async_copy(out.at[span], out_hbm.at[span], sems.at[i]))
        copies[-1].start()
    for copy in copies:
        copy.wait()


def products_of(turned, places, pairs, frames_all):
    sources, rows, width = turned.shape
    npairs = pairs.shape[1]
    depth = len(places[0]) * rows
    tiles = len(places) * width // TILE
    return pl.pallas_call(
        functools.partial(pairs_kernel, 1.0 / frames_all, places),
        out_shape=jax.ShapeDtypeStruct((npairs, TILE, 2 * TILE), jnp.bfloat16),
        in_specs=[
            pl.BlockSpec(memory_space=pltpu.SMEM),
            pl.BlockSpec(memory_space=pltpu.VMEM),
        ],
        out_specs=pl.BlockSpec(memory_space=pl.ANY),
        scratch_shapes=[
            pltpu.VMEM((tiles, TILE, depth), jnp.bfloat16),
            pltpu.VMEM((tiles, depth, 2 * TILE), jnp.bfloat16),
            pltpu.VMEM((npairs, TILE, 2 * TILE), jnp.bfloat16),
            pltpu.SemaphoreType.DMA((npairs // divisor(npairs, 32),)),
        ],
        compiler_params=pltpu.CompilerParams(vmem_limit_bytes=VMEM_LIMIT),
        name="pair_products",
    )(pairs, turned)


def turn_group(n_wide, n_time):
    middle = (n_wide // 2 + 1) * n_time - 1 + (n_time if n_wide > 2 else 0)
    plane = 2 * n_time
    others = [d for d in range(n_wide * n_time) if d != middle]
    return [middle] + sorted(others, key=lambda d: (-abs(d // plane - middle // plane), d))


def shards(voltages, channels, tile_pairs):
    n_wide = lax.axis_size("wide")
    n_time = lax.axis_size("tm")
    n_dev = n_wide * n_time
    in_dev = voltages.shape[0]
    frames_dev = voltages.shape[1] // NFFT
    count = channels.shape[0]
    per_dev = count // n_dev
    rows = 2 * frames_dev

    group = turn_group(n_wide, n_time)
    place = {d: j for j, d in enumerate(group)}
    order = [d * per_dev + c for d in group for c in range(per_dev)]

    spectra, pairs = spectra_of(voltages, channels, tile_pairs, order)
    turned = lax.all_to_all(
        spectra, ("wide", "tm"), split_axis=0, concat_axis=0, axis_index_groups=[group], tiled=True
    )
    turned = turned.reshape(n_dev, per_dev, rows, in_dev)
    results = []
    for c in range(per_dev):
        one = turned[:, c]
        places = [[place[w * n_time + t] for t in range(n_time)] for w in range(n_wide)]
        if in_dev % LANES:
            one = jnp.take(one, jnp.array([place[d] for d in range(n_dev)]), axis=0)
            one = one.reshape(n_wide, n_time, rows, in_dev).transpose(1, 2, 0, 3)
            one = one.reshape(n_time, rows, n_wide * in_dev)
            places = [list(range(n_time))]
        results.append(products_of(one, places, pairs, frames_dev * n_time))
    return jnp.stack(results)


def solution(mesh):
    return jax.shard_map(
        shards,
        mesh=mesh,
        in_specs=(P("wide", ("grp", "tm")), P(), P()),
        out_specs=P(("grp", "wide", "tm"), None, None, None),
        check_vma=False,
    )
```

```python
import functools
import math
import random

import jax
import jax.numpy as jnp
from jax import lax
from jax.experimental import pallas as pl
from jax.experimental.pallas import tpu as pltpu
from jax.sharding import PartitionSpec as P

TILE = 64
NFFT = 2048
LANES = 128
VMEM_LIMIT = 48 * 1024 * 1024


def divisor(n, most):
    return max(d for d in range(1, most + 1) if n % d == 0)


def cos_sin(phase):
    quarter = NFFT // 4
    turn = (phase + quarter // 2) // quarter
    x = (phase - turn * quarter).astype(jnp.float32) * (2.0 * math.pi / NFFT)
    y = x * x
    c = 1.0 + y * (-1 / 2 + y * (1 / 24 + y * (-1 / 720 + y * (1 / 40320))))
    s = x * (1.0 + y * (-1 / 6 + y * (1 / 120 + y * (-1 / 5040 + y * (1 / 362880)))))
    odd = (turn & 1) == 1
    cos = jnp.where(odd, s, c)
    sin = jnp.where(odd, c, s)
    cos = jnp.where(((turn + 1) & 2) == 2, -cos, cos)
    sin = jnp.where((turn & 2) == 2, -sin, sin)
    return cos, sin


def fill_table(order, chan_ref, table):
    count = table.shape[0] // 2
    rows = lax.broadcasted_iota(jnp.int32, (count, LANES), 0)
    chan = jnp.zeros((count, LANES), jnp.int32)
    for s in range(count):
        chan = jnp.where(rows == s, chan_ref[order[s]], chan)
    lane = lax.broadcasted_iota(jnp.int32, (count, LANES), 1)
    scale = 1.0 / math.sqrt(0.375 * NFFT)

    @pl.loop(0, NFFT // LANES)
    def _(j):
        start = pl.multiple_of(j * LANES, LANES)
        n = lane + start
        window = 0.5 - 0.5 * cos_sin(n[:8])[0]
        window = jnp.tile(window * scale, (count // 8, 1))
        cos, sin = cos_sin((chan * n) & (NFFT - 1))
        table[:count, pl.ds(start, LANES)] = (window * cos).astype(table.dtype)
        table[count:, pl.ds(start, LANES)] = (-window * sin).astype(table.dtype)


def spectra_kernel(
    order, chan_hbm, pairs_hbm, volt_hbm, out_ref, pairs_ref, chan, volt, table, spec, list_sems, sems
):
    frames, in_dev = volt.shape[:2]
    count = spec.shape[0]

    def frame(f):
        start = pl.multiple_of(f * NFFT, NFFT)
        return pltpu.make_async_copy(volt_hbm.at[:, pl.ds(start, NFFT)], volt.at[f], sems.at[f])

    chan_copy = pltpu.make_async_copy(chan_hbm, chan, list_sems.at[0])
    chan_copy.start()
    pairs_copy = pltpu.make_async_copy(pairs_hbm, pairs_ref, list_sems.at[1])
    pairs_copy.start()

    @pl.loop(0, frames)
    def _(f):
        frame(f).start()

    chan_copy.wait()
    pairs_copy.wait()
    fill_table(order, chan, table)

    def transform(f, several):
        for k in range(several):
            frame(f + k).wait()
        block = volt[pl.ds(f, several)].reshape(several * in_dev, NFFT)
        result = lax.dot_general(
            table[...], block, (((1,), (1,)), ((), ())), preferred_element_type=jnp.float32
        )
        for k in range(several):
            part = result[:, k * in_dev : (k + 1) * in_dev]
            spec[:, pl.ds(f + k, 1), :] = part[:count].reshape(count, 1, in_dev)
            spec[:, pl.ds(frames + f + k, 1), :] = part[count:].reshape(count, 1, in_dev)

    singles = min(frames, 2 + frames % 2)

    @pl.loop(0, singles)
    def _(f):
        transform(f, 1)

    @pl.loop(0, (frames - singles) // 2)
    def _(g):
        transform(singles + 2 * g, 2)

    out_ref[...] = spec[...].astype(out_ref.dtype)


def spectra_of(voltages, channels, tile_pairs, order):
    in_dev = voltages.shape[0]
    frames = voltages.shape[1] // NFFT
    count = channels.shape[0]
    lists = [pltpu.with_memory_space_constraint(x, pltpu.HBM) for x in (channels, tile_pairs.T)]
    return pl.pallas_call(
        functools.partial(spectra_kernel, order),
        out_shape=(
            jax.ShapeDtypeStruct((count, 2 * frames, in_dev), jnp.bfloat16),
            pltpu.SMEM(lists[1].shape, jnp.int32),
        ),
        in_specs=[pl.BlockSpec(memory_space=pl.ANY)] * 3,
        out_specs=(
            pl.BlockSpec(memory_space=pltpu.VMEM),
            pl.BlockSpec(memory_space=pltpu.SMEM),
        ),
        scratch_shapes=[
            pltpu.SMEM((count,), jnp.int32),
            pltpu.VMEM((frames, in_dev, NFFT), voltages.dtype),
            pltpu.VMEM((2 * count, NFFT), jnp.bfloat16),
            pltpu.VMEM((count, 2 * frames, in_dev), jnp.float32),
            pltpu.SemaphoreType.DMA((2,)),
            pltpu.SemaphoreType.DMA((frames,)),
        ],
        compiler_params=pltpu.CompilerParams(vmem_limit_bytes=VMEM_LIMIT),
        name="spectra",
    )(*lists, voltages)


def pairs_kernel(scale, places, pairs_ref, turned_ref, out_hbm, left, right, out, sems):
    sources, rows, width = turned_ref.shape
    times = len(places[0])
    half = rows // 2
    low = lax.broadcasted_iota(jnp.int32, (rows, LANES), 1) < TILE
    for w, place in enumerate(places):
        stack = []
        for t in range(times):
            x = turned_ref[place[t]].astype(jnp.float32)
            stack.append(x)
            m = jnp.concatenate([x[half:], -x[:half]], 0)
            for u in range(width // LANES):
                xu = x[:, u * LANES : (u + 1) * LANES]
                mu = m[:, u * LANES : (u + 1) * LANES]
                tile = (w * width + u * LANES) // TILE
                depth = slice(t * rows, (t + 1) * rows)
                first = jnp.where(low, xu, pltpu.roll(mu, TILE, 1))
                second = jnp.where(low, pltpu.roll(xu, TILE, 1), mu)
                right[tile, depth] = first.astype(right.dtype)
                right[tile + 1, depth] = second.astype(right.dtype)
        stack = jnp.concatenate(stack, 0)
        for u in range(width // LANES):
            turned = stack[:, u * LANES : (u + 1) * LANES].T.astype(left.dtype)
            tile = (w * width + u * LANES) // TILE
            left[tile] = turned[:TILE]
            left[tile + 1] = turned[TILE:]

    parts = sems.shape[0]
    step = out.shape[0] // parts
    copies = []
    for i in range(parts):
        span = slice(i * step, (i + 1) * step)
        for p in range(i * step, (i + 1) * step):
            product = lax.dot_general(
                left[pairs_ref[0, p]],
                right[pairs_ref[1, p]],
                (((1,), (0,)), ((), ())),
                preferred_element_type=jnp.float32,
            )
            out[p] = (product * scale).astype(out.dtype)
        copies.append(pltpu.make_async_copy(out.at[span], out_hbm.at[span], sems.at[i]))
        copies[-1].start()
    for copy in copies:
        copy.wait()


def products_of(turned, places, pairs, frames_all):
    sources, rows, width = turned.shape
    npairs = pairs.shape[1]
    depth = len(places[0]) * rows
    tiles = len(places) * width // TILE
    return pl.pallas_call(
        functools.partial(pairs_kernel, 1.0 / frames_all, places),
        out_shape=jax.ShapeDtypeStruct((npairs, TILE, 2 * TILE), jnp.bfloat16),
        in_specs=[
            pl.BlockSpec(memory_space=pltpu.SMEM),
            pl.BlockSpec(memory_space=pltpu.VMEM),
        ],
        out_specs=pl.BlockSpec(memory_space=pl.ANY),
        scratch_shapes=[
            pltpu.VMEM((tiles, TILE, depth), jnp.bfloat16),
            pltpu.VMEM((tiles, depth, 2 * TILE), jnp.bfloat16),
            pltpu.VMEM((npairs, TILE, 2 * TILE), jnp.bfloat16),
            pltpu.SemaphoreType.DMA((npairs // divisor(npairs, 32),)),
        ],
        compiler_params=pltpu.CompilerParams(vmem_limit_bytes=VMEM_LIMIT),
        name="pair_products",
    )(pairs, turned)


def turn_group(n_wide, n_time):
    middle = (n_wide // 2 + 1) * n_time - 1 + (n_time if n_wide > 2 else 0)
    others = [d for d in range(n_wide * n_time) if d != middle]
    random.Random(10).shuffle(others)
    return [middle] + others


def shards(voltages, channels, tile_pairs):
    n_wide = lax.axis_size("wide")
    n_time = lax.axis_size("tm")
    n_dev = n_wide * n_time
    in_dev = voltages.shape[0]
    frames_dev = voltages.shape[1] // NFFT
    count = channels.shape[0]
    per_dev = count // n_dev
    rows = 2 * frames_dev

    group = turn_group(n_wide, n_time)
    place = {d: j for j, d in enumerate(group)}
    order = [d * per_dev + c for d in group for c in range(per_dev)]

    spectra, pairs = spectra_of(voltages, channels, tile_pairs, order)
    turned = lax.all_to_all(
        spectra, ("wide", "tm"), split_axis=0, concat_axis=0, axis_index_groups=[group], tiled=True
    )
    turned = turned.reshape(n_dev, per_dev, rows, in_dev)
    results = []
    for c in range(per_dev):
        one = turned[:, c]
        places = [[place[w * n_time + t] for t in range(n_time)] for w in range(n_wide)]
        if in_dev % LANES:
            one = jnp.take(one, jnp.array([place[d] for d in range(n_dev)]), axis=0)
            one = one.reshape(n_wide, n_time, rows, in_dev).transpose(1, 2, 0, 3)
            one = one.reshape(n_time, rows, n_wide * in_dev)
            places = [list(range(n_time))]
        results.append(products_of(one, places, pairs, frames_dev * n_time))
    return jnp.stack(results)


def solution(mesh):
    return jax.shard_map(
        shards,
        mesh=mesh,
        in_specs=(P("wide", ("grp", "tm")), P(), P()),
        out_specs=P(("grp", "wide", "tm"), None, None, None),
        check_vma=False,
    )
```

```python
import functools
import math
import random

import jax
import jax.numpy as jnp
from jax import lax
from jax.experimental import pallas as pl
from jax.experimental.pallas import tpu as pltpu
from jax.sharding import PartitionSpec as P

TILE = 64
NFFT = 2048
LANES = 128
VMEM_LIMIT = 48 * 1024 * 1024


def divisor(n, most):
    return max(d for d in range(1, most + 1) if n % d == 0)


def cos_sin(phase):
    quarter = NFFT // 4
    turn = (phase + quarter // 2) // quarter
    x = (phase - turn * quarter).astype(jnp.float32) * (2.0 * math.pi / NFFT)
    y = x * x
    c = 1.0 + y * (-1 / 2 + y * (1 / 24 + y * (-1 / 720 + y * (1 / 40320))))
    s = x * (1.0 + y * (-1 / 6 + y * (1 / 120 + y * (-1 / 5040 + y * (1 / 362880)))))
    odd = (turn & 1) == 1
    cos = jnp.where(odd, s, c)
    sin = jnp.where(odd, c, s)
    cos = jnp.where(((turn + 1) & 2) == 2, -cos, cos)
    sin = jnp.where((turn & 2) == 2, -sin, sin)
    return cos, sin


def fill_table(order, chan_ref, table):
    count = table.shape[0] // 2
    rows = lax.broadcasted_iota(jnp.int32, (count, LANES), 0)
    chan = jnp.zeros((count, LANES), jnp.int32)
    for s in range(count):
        chan = jnp.where(rows == s, chan_ref[order[s]], chan)
    lane = lax.broadcasted_iota(jnp.int32, (count, LANES), 1)
    scale = 1.0 / math.sqrt(0.375 * NFFT)

    @pl.loop(0, NFFT // LANES)
    def _(j):
        start = pl.multiple_of(j * LANES, LANES)
        n = lane + start
        window = 0.5 - 0.5 * cos_sin(n[:8])[0]
        window = jnp.tile(window * scale, (count // 8, 1))
        cos, sin = cos_sin((chan * n) & (NFFT - 1))
        table[:count, pl.ds(start, LANES)] = (window * cos).astype(table.dtype)
        table[count:, pl.ds(start, LANES)] = (-window * sin).astype(table.dtype)


def spectra_kernel(
    order, chan_hbm, pairs_hbm, volt_hbm, out_ref, pairs_ref, chan, volt, table, spec, list_sems, sems
):
    frames, in_dev = volt.shape[:2]
    count = spec.shape[0]

    def frame(f):
        start = pl.multiple_of(f * NFFT, NFFT)
        return pltpu.make_async_copy(volt_hbm.at[:, pl.ds(start, NFFT)], volt.at[f], sems.at[f])

    chan_copy = pltpu.make_async_copy(chan_hbm, chan, list_sems.at[0])
    chan_copy.start()
    pairs_copy = pltpu.make_async_copy(pairs_hbm, pairs_ref, list_sems.at[1])

    @pl.loop(0, frames)
    def _(f):
        frame(f).start()

    pairs_copy.start()
    chan_copy.wait()
    fill_table(order, chan, table)

    def transform(f, several):
        for k in range(several):
            frame(f + k).wait()
        block = volt[pl.ds(f, several)].reshape(several * in_dev, NFFT)
        result = lax.dot_general(
            table[...], block, (((1,), (1,)), ((), ())), preferred_element_type=jnp.float32
        )
        for k in range(several):
            part = result[:, k * in_dev : (k + 1) * in_dev]
            spec[:, pl.ds(f + k, 1), :] = part[:count].reshape(count, 1, in_dev)
            spec[:, pl.ds(frames + f + k, 1), :] = part[count:].reshape(count, 1, in_dev)

    singles = min(frames, 2 + frames % 2)

    @pl.loop(0, singles)
    def _(f):
        transform(f, 1)

    @pl.loop(0, (frames - singles) // 2)
    def _(g):
        transform(singles + 2 * g, 2)

    out_ref[...] = spec[...].astype(out_ref.dtype)
    pairs_copy.wait()


def spectra_of(voltages, channels, tile_pairs, order):
    in_dev = voltages.shape[0]
    frames = voltages.shape[1] // NFFT
    count = channels.shape[0]
    lists = [pltpu.with_memory_space_constraint(x, pltpu.HBM) for x in (channels, tile_pairs.T)]
    return pl.pallas_call(
        functools.partial(spectra_kernel, order),
        out_shape=(
            jax.ShapeDtypeStruct((count, 2 * frames, in_dev), jnp.bfloat16),
            pltpu.SMEM(lists[1].shape, jnp.int32),
        ),
        in_specs=[pl.BlockSpec(memory_space=pl.ANY)] * 3,
        out_specs=(
            pl.BlockSpec(memory_space=pltpu.VMEM),
            pl.BlockSpec(memory_space=pltpu.SMEM),
        ),
        scratch_shapes=[
            pltpu.SMEM((count,), jnp.int32),
            pltpu.VMEM((frames, in_dev, NFFT), voltages.dtype),
            pltpu.VMEM((2 * count, NFFT), jnp.bfloat16),
            pltpu.VMEM((count, 2 * frames, in_dev), jnp.float32),
            pltpu.SemaphoreType.DMA((2,)),
            pltpu.SemaphoreType.DMA((frames,)),
        ],
        compiler_params=pltpu.CompilerParams(vmem_limit_bytes=VMEM_LIMIT),
        name="spectra",
    )(*lists, voltages)


def pairs_kernel(scale, places, pairs_ref, turned_ref, out_hbm, left, right, out, sems):
    sources, rows, width = turned_ref.shape
    times = len(places[0])
    half = rows // 2
    low = lax.broadcasted_iota(jnp.int32, (rows, LANES), 1) < TILE
    for w, place in enumerate(places):
        stack = []
        for t in range(times):
            x = turned_ref[place[t]].astype(jnp.float32)
            stack.append(turned_ref[place[t]])
            m = jnp.concatenate([x[half:], -x[:half]], 0)
            for u in range(width // LANES):
                xu = x[:, u * LANES : (u + 1) * LANES]
                mu = m[:, u * LANES : (u + 1) * LANES]
                tile = (w * width + u * LANES) // TILE
                depth = slice(t * rows, (t + 1) * rows)
                first = jnp.where(low, xu, pltpu.roll(mu, TILE, 1))
                second = jnp.where(low, pltpu.roll(xu, TILE, 1), mu)
                right[tile, depth] = first.astype(right.dtype)
                right[tile + 1, depth] = second.astype(right.dtype)
        stack = jnp.concatenate(stack, 0)
        for u in range(width // LANES):
            turned = stack[:, u * LANES : (u + 1) * LANES].T
            tile = (w * width + u * LANES) // TILE
            left[tile] = turned[:TILE]
            left[tile + 1] = turned[TILE:]

    parts = sems.shape[0]
    step = out.shape[0] // parts
    copies = []
    for i in range(parts):
        span = slice(i * step, (i + 1) * step)
        for p in range(i * step, (i + 1) * step):
            product = lax.dot_general(
                left[pairs_ref[0, p]],
                right[pairs_ref[1, p]],
                (((1,), (0,)), ((), ())),
                preferred_element_type=jnp.float32,
            )
            out[p] = (product * scale).astype(out.dtype)
        copies.append(pltpu.make_async_copy(out.at[span], out_hbm.at[span], sems.at[i]))
        copies[-1].start()
    for copy in copies:
        copy.wait()


def products_of(turned, places, pairs, frames_all):
    sources, rows, width = turned.shape
    npairs = pairs.shape[1]
    depth = len(places[0]) * rows
    tiles = len(places) * width // TILE
    return pl.pallas_call(
        functools.partial(pairs_kernel, 1.0 / frames_all, places),
        out_shape=jax.ShapeDtypeStruct((npairs, TILE, 2 * TILE), jnp.bfloat16),
        in_specs=[
            pl.BlockSpec(memory_space=pltpu.SMEM),
            pl.BlockSpec(memory_space=pltpu.VMEM),
        ],
        out_specs=pl.BlockSpec(memory_space=pl.ANY),
        scratch_shapes=[
            pltpu.VMEM((tiles, TILE, depth), jnp.bfloat16),
            pltpu.VMEM((tiles, depth, 2 * TILE), jnp.bfloat16),
            pltpu.VMEM((npairs, TILE, 2 * TILE), jnp.bfloat16),
            pltpu.SemaphoreType.DMA((npairs // divisor(npairs, 16),)),
        ],
        compiler_params=pltpu.CompilerParams(vmem_limit_bytes=VMEM_LIMIT),
        name="pair_products",
    )(pairs, turned)


def turn_group(n_wide, n_time):
    middle = (n_wide // 2 + 1) * n_time - 1 + (n_time if n_wide > 2 else 0)
    others = [d for d in range(n_wide * n_time) if d != middle]
    random.Random(10).shuffle(others)
    return [middle] + others


def shards(voltages, channels, tile_pairs):
    n_wide = lax.axis_size("wide")
    n_time = lax.axis_size("tm")
    n_dev = n_wide * n_time
    in_dev = voltages.shape[0]
    frames_dev = voltages.shape[1] // NFFT
    count = channels.shape[0]
    per_dev = count // n_dev
    rows = 2 * frames_dev

    group = turn_group(n_wide, n_time)
    place = {d: j for j, d in enumerate(group)}
    order = [d * per_dev + c for d in group for c in range(per_dev)]

    spectra, pairs = spectra_of(voltages, channels, tile_pairs, order)
    turned = lax.all_to_all(
        spectra, ("wide", "tm"), split_axis=0, concat_axis=0, axis_index_groups=[group], tiled=True
    )
    turned = turned.reshape(n_dev, per_dev, rows, in_dev)
    results = []
    for c in range(per_dev):
        one = turned[:, c]
        places = [[place[w * n_time + t] for t in range(n_time)] for w in range(n_wide)]
        if in_dev % LANES:
            one = jnp.take(one, jnp.array([place[d] for d in range(n_dev)]), axis=0)
            one = one.reshape(n_wide, n_time, rows, in_dev).transpose(1, 2, 0, 3)
            one = one.reshape(n_time, rows, n_wide * in_dev)
            places = [list(range(n_time))]
        results.append(products_of(one, places, pairs, frames_dev * n_time))
    return jnp.stack(results)


def solution(mesh):
    return jax.shard_map(
        shards,
        mesh=mesh,
        in_specs=(P("wide", ("grp", "tm")), P(), P()),
        out_specs=P(("grp", "wide", "tm"), None, None, None),
        check_vma=False,
    )
```

```python
import functools
import math
import random

import jax
import jax.numpy as jnp
from jax import lax
from jax.experimental import pallas as pl
from jax.experimental.pallas import tpu as pltpu
from jax.sharding import PartitionSpec as P

TILE = 64
NFFT = 2048
LANES = 128
VMEM_LIMIT = 48 * 1024 * 1024


def divisor(n, most):
    return max(d for d in range(1, most + 1) if n % d == 0)


def cos_sin(phase):
    quarter = NFFT // 4
    turn = (phase + quarter // 2) // quarter
    x = (phase - turn * quarter).astype(jnp.float32) * (2.0 * math.pi / NFFT)
    y = x * x
    c = 1.0 + y * (-1 / 2 + y * (1 / 24 + y * (-1 / 720 + y * (1 / 40320))))
    s = x * (1.0 + y * (-1 / 6 + y * (1 / 120 + y * (-1 / 5040 + y * (1 / 362880)))))
    odd = (turn & 1) == 1
    cos = jnp.where(odd, s, c)
    sin = jnp.where(odd, c, s)
    cos = jnp.where(((turn + 1) & 2) == 2, -cos, cos)
    sin = jnp.where((turn & 2) == 2, -sin, sin)
    return cos, sin


def fill_table(order, chan_ref, table):
    count = table.shape[0] // 2
    rows = lax.broadcasted_iota(jnp.int32, (count, LANES), 0)
    chan = jnp.zeros((count, LANES), jnp.int32)
    for s in range(count):
        chan = jnp.where(rows == s, chan_ref[order[s]], chan)
    lane = lax.broadcasted_iota(jnp.int32, (count, LANES), 1)
    scale = 1.0 / math.sqrt(0.375 * NFFT)

    @pl.loop(0, NFFT // LANES)
    def _(j):
        start = pl.multiple_of(j * LANES, LANES)
        n = lane + start
        window = 0.5 - 0.5 * cos_sin(n[:8])[0]
        window = jnp.tile(window * scale, (count // 8, 1))
        cos, sin = cos_sin((chan * n) & (NFFT - 1))
        table[:count, pl.ds(start, LANES)] = (window * cos).astype(table.dtype)
        table[count:, pl.ds(start, LANES)] = (-window * sin).astype(table.dtype)


def spectra_kernel(
    order, chan_hbm, pairs_hbm, volt_hbm, out_ref, pairs_ref, chan, volt, table, spec, list_sems, sems
):
    frames, in_dev = volt.shape[:2]
    count = spec.shape[0]

    def frame(f):
        start = pl.multiple_of(f * NFFT, NFFT)
        return pltpu.make_async_copy(volt_hbm.at[:, pl.ds(start, NFFT)], volt.at[f], sems.at[f])

    chan_copy = pltpu.make_async_copy(chan_hbm, chan, list_sems.at[0])
    chan_copy.start()
    pairs_copy = pltpu.make_async_copy(pairs_hbm, pairs_ref, list_sems.at[1])

    @pl.loop(0, frames)
    def _(f):
        frame(f).start()

    pairs_copy.start()
    chan_copy.wait()
    fill_table(order, chan, table)

    def transform(f, several):
        for k in range(several):
            frame(f + k).wait()
        results = [
            lax.dot_general(
                table[...],
                volt[f + k],
                (((1,), (1,)), ((), ())),
                preferred_element_type=jnp.float32,
            )
            for k in range(several)
        ]
        for k, part in enumerate(results):
            spec[:, pl.ds(f + k, 1), :] = part[:count].reshape(count, 1, in_dev)
            spec[:, pl.ds(frames + f + k, 1), :] = part[count:].reshape(count, 1, in_dev)

    singles = min(frames, 2 + frames % 2)

    @pl.loop(0, singles)
    def _(f):
        transform(f, 1)

    @pl.loop(0, (frames - singles) // 2)
    def _(g):
        transform(singles + 2 * g, 2)

    out_ref[...] = spec[...].astype(out_ref.dtype)
    pairs_copy.wait()


def spectra_of(voltages, channels, tile_pairs, order):
    in_dev = voltages.shape[0]
    frames = voltages.shape[1] // NFFT
    count = channels.shape[0]
    lists = [pltpu.with_memory_space_constraint(x, pltpu.HBM) for x in (channels, tile_pairs.T)]
    return pl.pallas_call(
        functools.partial(spectra_kernel, order),
        out_shape=(
            jax.ShapeDtypeStruct((count, 2 * frames, in_dev), jnp.bfloat16),
            pltpu.SMEM(lists[1].shape, jnp.int32),
        ),
        in_specs=[pl.BlockSpec(memory_space=pl.ANY)] * 3,
        out_specs=(
            pl.BlockSpec(memory_space=pltpu.VMEM),
            pl.BlockSpec(memory_space=pltpu.SMEM),
        ),
        scratch_shapes=[
            pltpu.SMEM((count,), jnp.int32),
            pltpu.VMEM((frames, in_dev, NFFT), voltages.dtype),
            pltpu.VMEM((2 * count, NFFT), jnp.bfloat16),
            pltpu.VMEM((count, 2 * frames, in_dev), jnp.float32),
            pltpu.SemaphoreType.DMA((2,)),
            pltpu.SemaphoreType.DMA((frames,)),
        ],
        compiler_params=pltpu.CompilerParams(vmem_limit_bytes=VMEM_LIMIT),
        name="spectra",
    )(*lists, voltages)


def pairs_kernel(scale, places, pairs_ref, turned_ref, out_hbm, left, right, out, sems):
    sources, rows, width = turned_ref.shape
    times = len(places[0])
    half = rows // 2
    low = lax.broadcasted_iota(jnp.int32, (rows, LANES), 1) < TILE
    for w, place in enumerate(places):
        stack = []
        for t in range(times):
            x = turned_ref[place[t]].astype(jnp.float32)
            stack.append(turned_ref[place[t]])
            m = jnp.concatenate([x[half:], -x[:half]], 0)
            for u in range(width // LANES):
                xu = x[:, u * LANES : (u + 1) * LANES]
                mu = m[:, u * LANES : (u + 1) * LANES]
                tile = (w * width + u * LANES) // TILE
                depth = slice(t * rows, (t + 1) * rows)
                first = jnp.where(low, xu, pltpu.roll(mu, TILE, 1))
                second = jnp.where(low, pltpu.roll(xu, TILE, 1), mu)
                right[tile, depth] = first.astype(right.dtype)
                right[tile + 1, depth] = second.astype(right.dtype)
        stack = jnp.concatenate(stack, 0)
        for u in range(width // LANES):
            turned = stack[:, u * LANES : (u + 1) * LANES].T
            tile = (w * width + u * LANES) // TILE
            left[tile] = turned[:TILE]
            left[tile + 1] = turned[TILE:]

    parts = sems.shape[0]
    step = out.shape[0] // parts
    copies = []
    for i in range(parts):
        span = slice(i * step, (i + 1) * step)
        for p in range(i * step, (i + 1) * step):
            product = lax.dot_general(
                left[pairs_ref[0, p]],
                right[pairs_ref[1, p]],
                (((1,), (0,)), ((), ())),
                preferred_element_type=jnp.float32,
            )
            out[p] = (product * scale).astype(out.dtype)
        copies.append(pltpu.make_async_copy(out.at[span], out_hbm.at[span], sems.at[i]))
        copies[-1].start()
    for copy in copies:
        copy.wait()


def products_of(turned, places, pairs, frames_all):
    sources, rows, width = turned.shape
    npairs = pairs.shape[1]
    depth = len(places[0]) * rows
    tiles = len(places) * width // TILE
    return pl.pallas_call(
        functools.partial(pairs_kernel, 1.0 / frames_all, places),
        out_shape=jax.ShapeDtypeStruct((npairs, TILE, 2 * TILE), jnp.bfloat16),
        in_specs=[
            pl.BlockSpec(memory_space=pltpu.SMEM),
            pl.BlockSpec(memory_space=pltpu.VMEM),
        ],
        out_specs=pl.BlockSpec(memory_space=pl.ANY),
        scratch_shapes=[
            pltpu.VMEM((tiles, TILE, depth), jnp.bfloat16),
            pltpu.VMEM((tiles, depth, 2 * TILE), jnp.bfloat16),
            pltpu.VMEM((npairs, TILE, 2 * TILE), jnp.bfloat16),
            pltpu.SemaphoreType.DMA((npairs // divisor(npairs, 16),)),
        ],
        compiler_params=pltpu.CompilerParams(vmem_limit_bytes=VMEM_LIMIT),
        name="pair_products",
    )(pairs, turned)


def turn_group(n_wide, n_time):
    middle = (n_wide // 2 + 1) * n_time - 1 + (n_time if n_wide > 2 else 0)
    others = [d for d in range(n_wide * n_time) if d != middle]
    random.Random(10).shuffle(others)
    return [middle] + others


def shards(voltages, channels, tile_pairs):
    n_wide = lax.axis_size("wide")
    n_time = lax.axis_size("tm")
    n_dev = n_wide * n_time
    in_dev = voltages.shape[0]
    frames_dev = voltages.shape[1] // NFFT
    count = channels.shape[0]
    per_dev = count // n_dev
    rows = 2 * frames_dev

    group = turn_group(n_wide, n_time)
    place = {d: j for j, d in enumerate(group)}
    order = [d * per_dev + c for d in group for c in range(per_dev)]

    spectra, pairs = spectra_of(voltages, channels, tile_pairs, order)
    turned = lax.all_to_all(
        spectra, ("wide", "tm"), split_axis=0, concat_axis=0, axis_index_groups=[group], tiled=True
    )
    turned = turned.reshape(n_dev, per_dev, rows, in_dev)
    results = []
    for c in range(per_dev):
        one = turned[:, c]
        places = [[place[w * n_time + t] for t in range(n_time)] for w in range(n_wide)]
        if in_dev % LANES:
            one = jnp.take(one, jnp.array([place[d] for d in range(n_dev)]), axis=0)
            one = one.reshape(n_wide, n_time, rows, in_dev).transpose(1, 2, 0, 3)
            one = one.reshape(n_time, rows, n_wide * in_dev)
            places = [list(range(n_time))]
        results.append(products_of(one, places, pairs, frames_dev * n_time))
    return jnp.stack(results)


def solution(mesh):
    return jax.shard_map(
        shards,
        mesh=mesh,
        in_specs=(P("wide", ("grp", "tm")), P(), P()),
        out_specs=P(("grp", "wide", "tm"), None, None, None),
        check_vma=False,
    )
```
